32 devices in a mesh: dp: 4 (over x, core), fy: 4 (over z), fx: 2 (over y).
Axes of the slice: x: 2, y: 2, z: 4, core: 2. Of those that a mesh axis runs over, the one named last changes fastest.
Arguments:
- fine_tokens: bfloat16 [4, 64, 64, 768], P('dp', 'fy', 'fx'), may hold values from -40 to 40
- parent: int32 [4, 64, 16], P('dp', 'fy', 'fx'), may hold values from 0 to 127, as said below
- coarse_tokens: bfloat16 [4, 128, 768], P('dp', 'fx'), may hold values from -6 to 6
- tile_level: int32 [4, 128], P('dp', 'fx'), may hold values from 0 to 2
- level_table: float32 [3, 768], replicated, may hold values from -3 to 3
- norm_gain: float32 [768], replicated, may hold values from 0.5 to 1.5
- qkv_weight: bfloat16 [768, 2304], replicated, may hold values from -7 to 7
- out_weight: bfloat16 [768, 768], replicated, may hold values from -0.21875 to 0.21875
- cotangent: bfloat16 [4, 64, 64, 768], P('dp', 'fy', 'fx'), may hold values from -6 to 6
Outputs:
- mixed: bfloat16 [4, 64, 64, 768], P('dp', 'fy', 'fx')
- grad_tokens: bfloat16 [4, 64, 64, 768], P('dp', 'fy', 'fx')
- grad_coarse: float32 [4, 128, 768], P('dp', 'fx')
- grad_qkv: float32 [768, 2304], P('dp')
- grad_out: float32 [768, 768], P('dp')
- grad_gain: float32 [768], P('dp')
- grad_level: float32 [3, 768], replicated
The draws below stay inside these ranges and needn't reach their ends.
Inputs may be any that keep to these rules, and one draw needn't show every extreme that they name: `parent`: each entry names a coarse token of the same frame; a token of level l is drawn with weight l + 1.
All inputs are finite; a program needn't handle non-finite values.
Results may differ from the reference program's by a relative error of at most 0.025.
Values may be sent and summed in bfloat16 or wider, within the bound.
No kernel may reach another device: no remote copies, remote signals or barrier semaphores. Data moves between devices by JAX's collectives and lax.ppermute only.
A program may use at most 128 MiB of HBM per device.

```python
import math
import jax
import jax.numpy as jnp
from jax import lax

D = 768
HEADS = 12
BLK = 4
LEVELS = 3
FRAMES = 4
NY = 64
NX = 64
NCOARSE = 128


def locate(bounds_row, picks_frame):
    return jnp.searchsorted(bounds_row, picks_frame, side='right').astype(jnp.int32)


def routing_tables(key):
    level_key = jax.random.fold_in(key, 11)
    pick_key = jax.random.fold_in(key, 12)
    levels = jax.random.randint(level_key, (FRAMES, NCOARSE), 0, LEVELS).astype(jnp.int32)
    bounds = jnp.cumsum(levels + 1, axis=1).astype(jnp.int32)
    totals = bounds[:, -1]
    picks = jax.random.randint(pick_key, (FRAMES, NY, NX // BLK), 0, totals[:, None, None]).astype(jnp.int32)
    parents = jax.vmap(locate)(bounds, picks)
    return (levels, parents)


def draw_parent(key, part):
    return routing_tables(key)[1]


def draw_tile_level(key, part):
    return routing_tables(key)[0]


def draw_fine_tokens(key, part):
    noise_key = jax.random.fold_in(key, 21)
    row_key = jax.random.fold_in(key, 22)
    column_key = jax.random.fold_in(key, 23)
    noise = jnp.clip(jax.random.normal(noise_key, (FRAMES, NY, NX, D), jnp.float32), -4.0, 4.0)
    row_scale = 0.3 * jnp.exp(jax.random.uniform(row_key, (FRAMES, NY, NX, 1), jnp.float32) * math.log(10.0))
    column_scale = 0.3 * jnp.exp(jax.random.uniform(column_key, (D,), jnp.float32) * math.log(10.0))
    values = noise * row_scale * column_scale
    return values.astype(jnp.bfloat16)


def draw_qkv_weight(key, part):
    base_key = jax.random.fold_in(key, 31)
    base = jnp.clip(jax.random.normal(base_key, (D, 3 * D), jnp.float32), -4.0, 4.0) * D ** (-0.5)
    return base.astype(jnp.bfloat16)


def block_levels(rng, dims, shards, low, high):
    def one(dim, parts):
        draws = jax.random.uniform(jax.random.fold_in(jax.random.fold_in(rng, 6), dim), (parts,), jnp.float32, low / len(shards), high / len(shards))
        return jnp.repeat(jnp.exp(draws), dims[dim] // parts).reshape((-1,) + (1,) * (len(dims) - dim - 1))

    gain = one(*shards[0])
    for cut in shards[1:]:
        gain = gain * one(*cut)
    return gain


def scatter_about(key, shape, spread, reach, cuts=(), dtype=jnp.bfloat16):
    loudness = block_levels(key, shape, cuts, -0.22, 0.18) if cuts else 1.0
    result = jax.random.normal(key, shape, jnp.float32) * spread * loudness
    return jnp.minimum(jnp.maximum(result, -reach), reach).astype(dtype)


def setup_inputs(seed: int = 0) -> dict:
    seeds = jax.random.split(jax.random.key(seed), 10)
    fine_tokens = draw_fine_tokens(jax.random.fold_in(seeds[9], 71), 0)
    parent = draw_parent(jax.random.fold_in(seeds[9], 71), 0)
    coarse_tokens = scatter_about(seeds[2], (FRAMES, NCOARSE, D), 1.0, 6.0, ((0, 4), (1, 2)))
    tile_level = draw_tile_level(jax.random.fold_in(seeds[9], 71), 0)
    level_table = scatter_about(seeds[4], (LEVELS, D), 0.5, 3.0, (), jnp.float32)
    norm_gain = jnp.clip(1.0 + 0.1 * jax.random.normal(seeds[5], (D,), jnp.float32), 0.5, 1.5)
    qkv_weight = draw_qkv_weight(jax.random.fold_in(seeds[9], 71), 0)
    out_weight = scatter_about(seeds[7], (D, D), D ** -0.5, 0.21875)
    cotangent = scatter_about(seeds[8], (FRAMES, NY, NX, D), 1.0, 6.0, ((0, 4), (1, 4), (2, 2)))
    return {"fine_tokens": fine_tokens, "parent": parent, "coarse_tokens": coarse_tokens, "tile_level": tile_level, "level_table": level_table, "norm_gain": norm_gain, "qkv_weight": qkv_weight, "out_weight": out_weight, "cotangent": cotangent}


def attend_forward(queries, key_rows, values, score_scale, query_form, key_form, score_form):
    scores = jnp.einsum(query_form + ',' + key_form + '->' + score_form, queries.astype(jnp.float32), key_rows.astype(jnp.float32)) * score_scale
    weights = jax.nn.softmax(scores, axis=-1)
    rounded = weights.astype(jnp.bfloat16)
    attended = jnp.einsum(score_form + ',' + key_form + '->' + query_form, rounded.astype(jnp.float32), values.astype(jnp.float32))
    return attended.astype(jnp.bfloat16)

def attend_backward(queries, key_rows, values, grad_out, score_scale, query_form, key_form, score_form):
    scores = jnp.einsum(query_form + ',' + key_form + '->' + score_form, queries.astype(jnp.float32), key_rows.astype(jnp.float32)) * score_scale
    weights = jax.nn.softmax(scores, axis=-1)
    rounded = weights.astype(jnp.bfloat16)
    grad_values = jnp.einsum(score_form + ',' + query_form + '->' + key_form, rounded.astype(jnp.float32), grad_out.astype(jnp.float32)).astype(jnp.bfloat16)
    grad_weights = jnp.einsum(query_form + ',' + key_form + '->' + score_form, grad_out.astype(jnp.float32), values.astype(jnp.float32))
    inner = lax.optimization_barrier(jnp.sum(weights * grad_weights, axis=-1, keepdims=True))
    grad_scores = (weights * (grad_weights - inner) * score_scale).astype(jnp.bfloat16)
    grad_queries = jnp.einsum(score_form + ',' + key_form + '->' + query_form, grad_scores.astype(jnp.float32), key_rows.astype(jnp.float32)).astype(jnp.bfloat16)
    grad_keys = jnp.einsum(score_form + ',' + query_form + '->' + key_form, grad_scores.astype(jnp.float32), queries.astype(jnp.float32)).astype(jnp.bfloat16)
    return (grad_queries, grad_keys, grad_values)

def split_heads(tensor, head_dim):
    return tensor.reshape(tensor.shape[0], tensor.shape[1], -1, head_dim)

def one_frame(fine_rows, parent_ids, coarse_rows, levels, cotangent_rows, level_table, norm_gain, qkv_weight, out_weight):
    half_width = D // 2
    head_dim = D // HEADS
    score_scale = head_dim ** (-0.5)
    summary = (coarse_rows.astype(jnp.float32) + level_table[levels]).astype(jnp.bfloat16)
    read_rows = summary[parent_ids].astype(jnp.float32)
    residual = fine_rows.astype(jnp.float32) + jnp.repeat(read_rows, BLK, axis=1)
    inv_rms = lax.rsqrt(lax.optimization_barrier(jnp.mean(residual * residual, axis=-1, keepdims=True)) + 1e-06)
    normed_pre = residual * inv_rms
    normed = (normed_pre * norm_gain).astype(jnp.bfloat16)
    flat_normed = normed.reshape(NY * NX, D)
    projected = jnp.dot(flat_normed, qkv_weight, preferred_element_type=jnp.float32).astype(jnp.bfloat16).reshape(NY, NX, 3 * D)
    row_query = split_heads(projected[..., 0:half_width], head_dim)
    column_query = split_heads(projected[..., half_width:D], head_dim)
    row_key = split_heads(projected[..., D:D + half_width], head_dim)
    column_key = split_heads(projected[..., D + half_width:2 * D], head_dim)
    row_value = split_heads(projected[..., 2 * D:2 * D + half_width], head_dim)
    column_value = split_heads(projected[..., 2 * D + half_width:3 * D], head_dim)
    row_out = attend_forward(row_query, row_key, row_value, score_scale, 'bqhd', 'bkhd', 'bhqk')
    column_out = attend_forward(column_query, column_key, column_value, score_scale, 'qbhd', 'kbhd', 'bhqk')
    attended = jnp.concatenate([row_out.reshape(NY, NX, half_width), column_out.reshape(NY, NX, half_width)], axis=-1)
    flat_att = attended.reshape(NY * NX, D)
    out_proj = jnp.dot(flat_att, out_weight, preferred_element_type=jnp.float32)
    mixed = (residual + out_proj.reshape(NY, NX, D)).astype(jnp.bfloat16)
    flat_cot = cotangent_rows.reshape(NY * NX, D)
    grad_att = jnp.dot(flat_cot, out_weight.T, preferred_element_type=jnp.float32).astype(jnp.bfloat16).reshape(NY, NX, D)
    grad_out_weight = jnp.dot(flat_att.T, flat_cot, preferred_element_type=jnp.float32)
    row_grads = attend_backward(row_query, row_key, row_value, split_heads(grad_att[..., 0:half_width], head_dim), score_scale, 'bqhd', 'bkhd', 'bhqk')
    column_grads = attend_backward(column_query, column_key, column_value, split_heads(grad_att[..., half_width:D], head_dim), score_scale, 'qbhd', 'kbhd', 'bhqk')
    pieces = []
    for which in range(3):
        pieces.append(row_grads[which].reshape(NY, NX, half_width))
        pieces.append(column_grads[which].reshape(NY, NX, half_width))
    grad_projected = jnp.concatenate(pieces, axis=-1).reshape(NY * NX, 3 * D)
    grad_normed = jnp.dot(grad_projected, qkv_weight.T, preferred_element_type=jnp.float32)
    grad_qkv_weight = jnp.dot(flat_normed.T, grad_projected, preferred_element_type=jnp.float32)
    flat_pre = normed_pre.reshape(NY * NX, D)
    grad_gain = lax.optimization_barrier(jnp.sum(grad_normed * flat_pre, axis=0))
    grad_pre = grad_normed * norm_gain
    flat_inv = inv_rms.reshape(NY * NX, 1)
    grad_residual = flat_inv * (grad_pre - flat_pre * lax.optimization_barrier(jnp.mean(grad_pre * flat_pre, axis=-1, keepdims=True))) + flat_cot.astype(jnp.float32)
    grad_fine = grad_residual.astype(jnp.bfloat16).reshape(NY, NX, D)
    block_grad = grad_residual.reshape(NY, NX // BLK, BLK, D).sum(axis=2).reshape(-1, D)
    grad_coarse = jax.ops.segment_sum(block_grad, parent_ids.reshape(-1), num_segments=NCOARSE)
    grad_level = jax.ops.segment_sum(grad_coarse, levels, num_segments=LEVELS)
    return (mixed, grad_fine, grad_coarse, grad_qkv_weight, grad_out_weight, grad_gain, grad_level)

def reference(fine_tokens, parent, coarse_tokens, tile_level, level_table, norm_gain, qkv_weight, out_weight, cotangent):

    def frame_step(totals, frame_data):
        fine_rows, parent_ids, coarse_rows, levels, cotangent_rows = frame_data
        results = one_frame(fine_rows, parent_ids, coarse_rows, levels, cotangent_rows, level_table, norm_gain, qkv_weight, out_weight)
        totals = (totals[0] + results[3], totals[1] + results[4], totals[2] + results[5], totals[3] + results[6])
        return (totals, (results[0], results[1], results[2]))
    initial = (jnp.zeros((D, 3 * D), jnp.float32), jnp.zeros((D, D), jnp.float32), jnp.zeros((D,), jnp.float32), jnp.zeros((LEVELS, D), jnp.float32))
    totals, stacked = lax.scan(frame_step, initial, (fine_tokens, parent, coarse_tokens, tile_level, cotangent))
    grad_scale = 1.0 / math.sqrt(FRAMES * NY * NX)
    return (stacked[0], stacked[1], stacked[2], totals[0] * grad_scale, totals[1] * grad_scale, totals[2] * grad_scale, totals[3] * grad_scale)
```

```python
import functools
import math

import jax
import jax.numpy as jnp
from jax import lax
from jax.experimental import pallas as pl
from jax.experimental.pallas import tpu as pltpu
from jax.sharding import PartitionSpec as P

HEADS = 12
BLK = 4
LEVELS = 3
BASE = 128
PAD = 8
GROUP = 256
MIB = 1 << 20
F32 = jnp.float32
BF16 = jnp.bfloat16


def is_power(n):
    return n & (n - 1) == 0


def idiv(x, k):
    return x >> (k.bit_length() - 1) if is_power(k) else lax.div(x, jnp.int32(k))


def imod(x, k):
    return x & (k - 1) if is_power(k) else lax.rem(x, jnp.int32(k))


def iota(shape, dim):
    return lax.broadcasted_iota(jnp.int32, shape, dim)


def mm(a, b, ca=1, cb=0):
    return lax.dot_general(a, b, (((ca,), (cb,)), ((), ())), preferred_element_type=F32)


def xor_send(x, axis, s):
    n = lax.axis_size(axis)
    return lax.ppermute(x, axis, [(i, i ^ s) for i in range(n)])


def call(body, outs, scratch, cost, name, *args):
    return pl.pallas_call(
        body,
        out_shape=outs,
        in_specs=[pl.BlockSpec(memory_space=pltpu.VMEM)] * len(args),
        out_specs=[pl.BlockSpec(memory_space=pltpu.VMEM)] * len(outs),
        scratch_shapes=scratch,
        compiler_params=pltpu.CompilerParams(vmem_limit_bytes=48 * MIB),
        cost_estimate=pl.CostEstimate(flops=cost[0], bytes_accessed=cost[1], transcendentals=0),
        name=name,
    )(*args)


class Sizes:
    def __init__(self, rows, columns, width, owned):
        self.nx, self.ny, self.nd = (lax.axis_size(a) for a in ("fx", "fy", "dp"))
        self.rows, self.columns, self.width, self.owned = rows, columns, width, owned
        self.tokens = rows * columns
        self.blocks = self.tokens // BLK
        self.half = width // 2
        self.coarse = owned * self.nx
        self.row_tokens = self.tokens // self.nx
        self.col_lines = columns // self.ny
        self.col_tokens = self.tokens // self.ny


def place_col(sz, group, transposed=False):
    shape = (sz.tokens, sz.col_tokens) if transposed else (sz.col_tokens, sz.tokens)
    piece, own = (1, 0) if transposed else (0, 1)
    there, here = iota(shape, piece), iota(shape, own)
    want = imod(there, sz.rows) * sz.columns + idiv(there, sz.rows) + group * sz.col_lines
    return (want == here).astype(F32).astype(BF16)


def digits(parent_ref):
    ids = parent_ref[...]
    lo, hi = imod(ids, BASE), idiv(ids, BASE)
    row = iota((PAD, ids.shape[1]), 0)
    both = jnp.where(row == 0, lo, jnp.where(row == 1, hi, 0))
    return both.astype(F32).astype(BF16)


def onehot_ids(rows, coarse):
    rows = rows.astype(F32)
    ids = (rows[0:1, :] + rows[1:2, :] * BASE).astype(jnp.int32)
    return (iota((coarse, ids.shape[1]), 0) == ids).astype(F32).astype(BF16)


def own_onehot(sz, parent_ref):
    spread = idiv(iota((sz.blocks, sz.tokens), 1), BLK) == iota((sz.blocks, sz.tokens), 0)
    rows = mm(digits(parent_ref), spread.astype(F32).astype(BF16))
    return onehot_ids(rows, sz.coarse)


def fill_summary(sz, table, refs):
    mx = lax.axis_index("fx")
    for s, ref in enumerate(refs):
        start = pl.multiple_of((mx ^ s) * sz.owned, sz.owned)
        table[pl.ds(start, sz.owned), :] = ref[...]


def prep_kernel(sz, fine, parent, *outs):
    mx, my = lax.axis_index("fx"), lax.axis_index("fy")
    both = digits(parent)

    def finish(out, tokens, block):
        pick = (block == iota((sz.blocks, tokens), 0)).astype(F32).astype(BF16)
        out[tokens : tokens + PAD, :] = jnp.zeros((PAD, sz.width), BF16)
        out[tokens : tokens + PAD, 0:tokens] = mm(both, pick).astype(BF16)

    for s in range(sz.ny):
        group, out, n = my ^ s, outs[sz.nx + s], sz.col_tokens
        out[0:n, :] = mm(place_col(sz, group), fine[...]).astype(BF16)
        t = iota((sz.blocks, n), 1)
        column = idiv(t, sz.rows) + group * sz.col_lines
        finish(out, n, imod(t, sz.rows) * (sz.columns // BLK) + idiv(column, BLK))
    for s in range(sz.nx):
        start, out, n = (mx ^ s) * sz.row_tokens, outs[s], sz.row_tokens
        out[0:n, :] = fine[pl.ds(pl.multiple_of(start, n), n), :]
        finish(out, n, idiv(iota((sz.blocks, n), 1) + start, BLK))


def grad_att_kernel(sz, cot, weight, parent, *refs):
    outs, (total,), (held,) = refs[: sz.nx + sz.ny], refs[sz.nx + sz.ny : -1], refs[-1:]
    mx, my = lax.axis_index("fx"), lax.axis_index("fy")
    held[...] = mm(cot[...], weight[...], 1, 1).astype(BF16)
    for s in range(sz.ny):
        picked = mm(place_col(sz, my ^ s), held[:, sz.half :])
        outs[sz.nx + s][...] = picked.astype(BF16)
    for s in range(sz.nx):
        start = pl.multiple_of((mx ^ s) * sz.row_tokens, sz.row_tokens)
        outs[s][...] = held[pl.ds(start, sz.row_tokens), 0 : sz.half]
    total[...] = mm(own_onehot(sz, parent), cot[...])


def attend_kernel(sz, n, seg, offset, *refs):
    refs = list(refs)

    def take(count):
        out = refs[:count]
        del refs[:count]
        return out

    pieces, grads, tables = take(n), take(n), take(sz.nx)
    gain_ref, weight = take(2)
    o_outs, f_outs = take(n), take(n)
    keep, send, sums, gain_sum = take(4)
    table, xs, nb, gs, qkv, dqkv, os, fs, dw = take(9)
    tp, width, half = sz.tokens // n, sz.width, sz.half
    head = width // HEADS
    scale = head**-0.5
    lines = max(1, min(GROUP // (seg * n), tp // seg))
    part = lines * seg
    size = part * n
    groups = tp // part
    gain = gain_ref[...]

    fill_summary(sz, table, tables)
    onehots = []
    for p in range(n):
        onehot = onehot_ids(pieces[p][tp : tp + PAD, 0:tp], sz.coarse)
        onehots.append(onehot)
        x = pieces[p][0:tp, :].astype(F32) + mm(onehot, table[...], 0, 0)
        for g in range(groups):
            at = g * size + p * part
            xs[at : at + part, :] = x[g * part : (g + 1) * part, :]
            gs[at : at + part, :] = grads[p][g * part : (g + 1) * part, :]
    x = xs[...]
    inv = lax.rsqrt(jnp.mean(x * x, axis=-1, keepdims=True) + 1e-06)
    nb[...] = (x * inv * gain).astype(BF16)
    for which in range(3):
        lo = which * width + offset
        qkv[:, which * half : (which + 1) * half] = mm(
            nb[...], weight[:, lo : lo + half]
        ).astype(BF16)

    row_line = idiv(imod(iota((size, size), 0), part), seg)
    col_line = idiv(imod(iota((size, size), 1), part), seg)
    bias = jnp.where(row_line == col_line, 0.0, -1e30).astype(F32)
    pair = 2 * head
    first = iota((size, pair), 1) < head
    lane = iota((1, pair), 1) < head
    masks = (lane.astype(F32).astype(BF16), 1 - lane.astype(F32).astype(BF16))
    for g in range(groups):
        at = slice(g * size, (g + 1) * size)
        for h in range(half // pair):
            cols = [slice(w * half + h * pair, w * half + (h + 1) * pair) for w in range(3)]
            q, k, v = (qkv[at, c] for c in cols)
            go = gs[at, cols[0]]
            res = []
            for m in masks:
                s = mm(q * m, k, 1, 1) * scale + bias
                e = jnp.exp(s - jnp.max(s, axis=-1, keepdims=True))
                w = e * (1.0 / jnp.sum(e, axis=-1, keepdims=True))
                wb = w.astype(BF16)
                gw = mm(go * m, v, 1, 1)
                inner = jnp.sum(w * gw, axis=-1, keepdims=True)
                ds = (w * (gw - inner) * scale).astype(BF16)
                res.append((mm(wb, v), mm(ds, k), mm(ds, q, 0, 0), mm(wb, go, 0, 0)))
            out = [jnp.where(first, a, b).astype(BF16) for a, b in zip(*res)]
            os[at, cols[0]] = out[0]
            for c, d in zip(cols, out[1:]):
                dqkv[at, c] = d

    gn = jnp.zeros((sz.tokens, width), F32)
    for which in range(3):
        lo = which * width + offset
        gn += mm(
            dqkv[:, which * half : (which + 1) * half], weight[:, lo : lo + half], 1, 1
        )
    pre = xs[...] * inv
    gain_sum[...] = jnp.sum(gn * pre, axis=0, keepdims=True)
    gp = gn * gain
    fs[...] = (inv * (gp - pre * jnp.mean(gp * pre, axis=-1, keepdims=True))).astype(BF16)
    total = jnp.zeros((sz.coarse, width), F32)
    for p in range(n):
        for g in range(groups):
            at = g * size + p * part
            o_outs[p][g * part : (g + 1) * part, :] = os[at : at + part, :]
            f_outs[p][g * part : (g + 1) * part, :] = fs[at : at + part, :]
        total += mm(onehots[p], f_outs[p][...])
    sums[...] = total
    dw[...] = mm(nb[...], dqkv[...], 0, 0)
    split_blocks(sz, dw, keep, send)


def split_blocks(sz, dw, keep, send):
    rows = dw.shape[0] // sz.nd
    bit = lax.axis_index("dp") & 1
    for j in range(sz.nd // 2):
        for out, b in ((keep, bit), (send, 1 - bit)):
            start = pl.multiple_of((2 * j + b) * rows, rows)
            out[j * rows : (j + 1) * rows, :] = dw[pl.ds(start, rows), :].astype(BF16)


def mix_kernel(sz, fine, parent, cot, weight, *refs):
    tables, refs = refs[: sz.nx], refs[sz.nx :]
    row_out, refs = refs[: sz.nx], refs[sz.nx :]
    col_out, refs = refs[: sz.ny], refs[sz.ny :]
    mixed, keep, send, table, att, dw = refs
    my = lax.axis_index("fy")
    mx = lax.axis_index("fx")
    fill_summary(sz, table, tables)
    for s in range(sz.nx):
        start = pl.multiple_of((mx ^ s) * sz.row_tokens, sz.row_tokens)
        att[pl.ds(start, sz.row_tokens), 0 : sz.half] = row_out[s][...]
    col = jnp.zeros((sz.tokens, sz.half), F32)
    for s in range(sz.ny):
        col += mm(place_col(sz, my ^ s, True), col_out[s][...])
    att[:, sz.half :] = col.astype(BF16)
    x = fine[...].astype(F32) + mm(own_onehot(sz, parent), table[...], 0, 0)
    mixed[...] = (x + mm(att[...], weight[...])).astype(BF16)
    dw[...] = mm(att[...], cot[...], 0, 0)
    split_blocks(sz, dw, keep, send)


def tokens_kernel(sz, cot, *refs):
    rows, refs = refs[: sz.nx], refs[sz.nx :]
    cols, refs = refs[: sz.ny], refs[sz.ny :]
    out, held = refs
    my, mx = lax.axis_index("fy"), lax.axis_index("fx")
    for s in range(sz.nx):
        start = pl.multiple_of((mx ^ s) * sz.row_tokens, sz.row_tokens)
        held[pl.ds(start, sz.row_tokens), :] = rows[s][...]
    total = held[...].astype(F32) + cot[...].astype(F32)
    for s in range(sz.ny):
        total += mm(place_col(sz, my ^ s, True), cols[s][...])
    out[...] = total.astype(BF16)


def add(a, *others):
    out = a.astype(F32)
    for b in others:
        out = out + b.astype(F32)
    return out.astype(BF16)


def pick(stack, index):
    return lax.dynamic_index_in_dim(stack, index, 0, keepdims=False)


def reduce_weight(keep, send, nd):
    md = lax.axis_index("dp")
    value = add(keep, xor_send(send, "dp", 1))
    rows, step = keep.shape[0] // (nd // 2), 2
    while step < nd:
        bit = (md // step) & 1
        parts = value.reshape(-1, 2, rows, value.shape[-1])
        other = lax.dynamic_index_in_dim(parts, 1 - bit, 1, keepdims=False)
        mine = lax.dynamic_index_in_dim(parts, bit, 1, keepdims=False)
        value = add(mine, xor_send(other, "dp", step))
        value = value.reshape(-1, value.shape[-1])
        step *= 2
    for axis in ("fx", "fy"):
        n, me = lax.axis_size(axis), lax.axis_index(axis)
        parts = value.reshape(n, -1, value.shape[-1])
        got = [xor_send(pick(parts, me ^ s), axis, s) for s in range(1, n)]
        value = add(pick(parts, me), *got)
    for axis in ("fy", "fx"):
        n, me = lax.axis_size(axis), lax.axis_index(axis)
        got = [value] + [xor_send(value, axis, s) for s in range(1, n)]
        ordered = []
        for j in range(n):
            piece = got[j]
            for m in range(1, n):
                piece = jnp.where(me == m, got[j ^ m], piece)
            ordered.append(piece)
        value = jnp.concatenate(ordered, axis=0)
    return value


def local(
    fine_tokens,
    parent,
    coarse_tokens,
    tile_level,
    level_table,
    norm_gain,
    qkv_weight,
    out_weight,
    cotangent,
):
    frames, rows, columns, width = fine_tokens.shape
    owned = coarse_tokens.shape[1]
    sz = Sizes(rows, columns, width, owned)
    nx, ny, nd, tokens, half, coarse = sz.nx, sz.ny, sz.nd, sz.tokens, sz.half, sz.coarse
    if frames != 1 or not all(is_power(n) for n in (nx, ny, nd)):
        raise ValueError("unsupported mesh")

    def out(shape, dtype=BF16):
        return jax.ShapeDtypeStruct(shape, dtype)

    def vmem(shape, dtype=BF16):
        return pltpu.VMEM(shape, dtype)

    fine = fine_tokens.reshape(tokens, width)
    cot = cotangent.reshape(tokens, width)
    parents = parent.reshape(1, sz.blocks)
    gain = norm_gain.reshape(1, width)
    tr, tc = sz.row_tokens, sz.col_tokens

    sent = call(
        functools.partial(prep_kernel, sz),
        [out((tr + PAD, width))] * nx + [out((tc + PAD, width))] * ny,
        [],
        (2 * tokens * tokens * width, 6 * tokens * width),
        "prep",
        fine,
        parents,
    )
    level_onehot = (tile_level[0, :, None] == jnp.arange(LEVELS, dtype=jnp.int32)).astype(F32)
    level_add = jnp.sum(level_onehot[:, :, None] * level_table[None, :, :], axis=1)
    summary = (coarse_tokens[0].astype(F32) + level_add).astype(BF16)
    col_in = [sent[nx]] + [xor_send(sent[nx + s], "fy", s) for s in range(1, ny)]
    row_in = [sent[0]] + [xor_send(sent[s], "fx", s) for s in range(1, nx)]
    tables = [summary] + [xor_send(summary, "fx", s) for s in range(1, nx)]

    *gsent, cot_sums = call(
        functools.partial(grad_att_kernel, sz),
        [out((tr, half))] * nx + [out((tc, half))] * ny + [out((coarse, width), F32)],
        [vmem((tokens, width))],
        (2 * tokens * width * 2 * width, 6 * tokens * width),
        "grad_att",
        cot,
        out_weight,
        parents,
    )
    col_g = [gsent[nx]] + [xor_send(gsent[nx + s], "fy", s) for s in range(1, ny)]
    row_g = [gsent[0]] + [xor_send(gsent[s], "fx", s) for s in range(1, nx)]

    def attend(n, seg, offset, pieces, grads, name):
        tp = tokens // n
        res = call(
            functools.partial(attend_kernel, sz, n, seg, offset),
            [out((tp, half))] * n
            + [out((tp, width))] * n
            + [out((width // 2, 3 * half))] * 2
            + [out((coarse, width), F32), out((1, width), F32)],
            [
                vmem((coarse, width)),
                vmem((tokens, width), F32),
                vmem((tokens, width)),
                vmem((tokens, half)),
                vmem((tokens, 3 * half)),
                vmem((tokens, 3 * half)),
                vmem((tokens, half)),
                vmem((tokens, width)),
                vmem((width, 3 * half), F32),
            ],
            (10 * tokens * width * 3 * width, 12 * tokens * width),
            name,
            *pieces,
            *grads,
            *tables,
            gain,
            qkv_weight,
        )
        return res[:n], res[n : 2 * n], res[2 * n : 2 * n + 2], res[-2], res[-1]

    row_o, row_f, row_w, row_sums, row_gain = attend(nx, columns, 0, row_in, row_g, "row_heads")
    row_o = [row_o[0]] + [xor_send(row_o[s], "fx", s) for s in range(1, nx)]
    row_f = [row_f[0]] + [xor_send(row_f[s], "fx", s) for s in range(1, nx)]
    row_weight = reduce_weight(*row_w, nd)
    col_o, col_f, col_w, col_sums, col_gain = attend(ny, rows, half, col_in, col_g, "col_heads")
    col_o = [col_o[0]] + [xor_send(col_o[s], "fy", s) for s in range(1, ny)]
    col_f = [col_f[0]] + [xor_send(col_f[s], "fy", s) for s in range(1, ny)]
    col_weight = reduce_weight(*col_w, nd)

    mixed, *out_w = call(
        functools.partial(mix_kernel, sz),
        [out((tokens, width))] + [out((width // 2, width))] * 2,
        [vmem((coarse, width)), vmem((tokens, width)), vmem((width, width), F32)],
        (4 * tokens * width * width, 10 * tokens * width),
        "mix",
        fine,
        parents,
        cot,
        out_weight,
        *tables,
        *row_o,
        *col_o,
    )
    out_weight_sum = reduce_weight(*out_w, nd)

    sums = (cot_sums + row_sums + col_sums).reshape(nx, owned, width)
    mx = lax.axis_index("fx")
    got = [xor_send(pick(sums, mx ^ s).astype(BF16), "fx", s) for s in range(1, nx)]
    owner_sum = pick(sums, mx)
    for piece in got:
        owner_sum = owner_sum + piece.astype(F32)
    level_part = jnp.sum(level_onehot[:, :, None] * owner_sum[:, None, :], axis=0)
    sent_sum = owner_sum.astype(BF16)
    terms = [sent_sum.astype(F32)] + [
        xor_send(sent_sum, "fy", s).astype(F32) for s in range(1, ny)
    ]
    while len(terms) > 1:
        terms = [a + b for a, b in zip(terms[0::2], terms[1::2])]
    grad_coarse = terms[0]

    small = jnp.concatenate(
        [level_part, row_gain + col_gain, jnp.zeros((8 - LEVELS - 1, width), F32)], axis=0
    )
    for axis in ("dp", "fx", "fy"):
        step = 1
        while step < lax.axis_size(axis):
            small = small + xor_send(small, axis, step)
            step *= 2

    grad_tokens = call(
        functools.partial(tokens_kernel, sz),
        [out((tokens, width))],
        [vmem((tokens, width))],
        (2 * tokens * tokens * width, 8 * tokens * width),
        "grad_tokens",
        cot,
        *row_f,
        *col_f,
    )[0]

    scale = 1.0 / math.sqrt(tokens * nd * nx * ny)
    parts = []
    for which in range(3):
        cols = slice(which * half, (which + 1) * half)
        parts += [row_weight[:, cols], col_weight[:, cols]]
    grad_qkv = jnp.concatenate(parts, axis=1).astype(F32) * scale
    gain_rows = small[LEVELS].reshape(nd, width // nd)
    return (
        mixed.reshape(fine_tokens.shape),
        grad_tokens.reshape(fine_tokens.shape),
        grad_coarse.reshape(1, owned, width),
        grad_qkv,
        out_weight_sum.astype(F32) * scale,
        pick(gain_rows, lax.axis_index("dp")) * scale,
        small[:LEVELS] * scale,
    )


def solution(mesh):
    return jax.shard_map(
        local,
        mesh=mesh,
        in_specs=(
            P("dp", "fy", "fx", None),
            P("dp", "fy", "fx"),
            P("dp", "fx", None),
            P("dp", "fx"),
            P(),
            P(),
            P(),
            P(),
            P("dp", "fy", "fx", None),
        ),
        out_specs=(
            P("dp", "fy", "fx", None),
            P("dp", "fy", "fx", None),
            P("dp", "fx", None),
            P("dp", None),
            P("dp", None),
            P("dp"),
            P(),
        ),
        check_vma=False,
    )
```

```python
import functools
import math

import jax
import jax.numpy as jnp
from jax import lax
from jax.experimental import pallas as pl
from jax.experimental.pallas import tpu as pltpu
from jax.sharding import PartitionSpec as P

HEADS = 12
BLK = 4
LEVELS = 3
BASE = 128
PAD = 8
GROUP = 256
MIB = 1 << 20
F32 = jnp.float32
BF16 = jnp.bfloat16


def is_power(n):
    return n & (n - 1) == 0


def idiv(x, k):
    return x >> (k.bit_length() - 1) if is_power(k) else lax.div(x, jnp.int32(k))


def imod(x, k):
    return x & (k - 1) if is_power(k) else lax.rem(x, jnp.int32(k))


def iota(shape, dim):
    return lax.broadcasted_iota(jnp.int32, shape, dim)


def mm(a, b, ca=1, cb=0):
    return lax.dot_general(a, b, (((ca,), (cb,)), ((), ())), preferred_element_type=F32)


def xor_send(x, axis, s):
    n = lax.axis_size(axis)
    return lax.ppermute(x, axis, [(i, i ^ s) for i in range(n)])


def call(body, outs, scratch, cost, name, *args):
    return pl.pallas_call(
        body,
        out_shape=outs,
        scratch_shapes=scratch,
        compiler_params=pltpu.CompilerParams(vmem_limit_bytes=32 * MIB),
        cost_estimate=pl.CostEstimate(flops=cost[0], bytes_accessed=cost[1], transcendentals=0),
        name=name,
    )(*args)


class Sizes:
    def __init__(self, rows, columns, width, owned):
        self.nx, self.ny, self.nd = (lax.axis_size(a) for a in ("fx", "fy", "dp"))
        self.rows, self.columns, self.width, self.owned = rows, columns, width, owned
        self.tokens = rows * columns
        self.blocks = self.tokens // BLK
        self.half = width // 2
        self.coarse = owned * self.nx
        self.row_tokens = self.tokens // self.nx
        self.col_lines = columns // self.ny
        self.col_tokens = self.tokens // self.ny


def place_col(sz, group, transposed=False):
    shape = (sz.tokens, sz.col_tokens) if transposed else (sz.col_tokens, sz.tokens)
    piece, own = (1, 0) if transposed else (0, 1)
    there, here = iota(shape, piece), iota(shape, own)
    want = imod(there, sz.rows) * sz.columns + idiv(there, sz.rows) + group * sz.col_lines
    return (want == here).astype(F32).astype(BF16)


def digits(parent_ref):
    ids = parent_ref[...]
    lo, hi = imod(ids, BASE), idiv(ids, BASE)
    row = iota((PAD, ids.shape[1]), 0)
    both = jnp.where(row == 0, lo, jnp.where(row == 1, hi, 0))
    return both.astype(F32).astype(BF16)


def onehot_ids(rows, coarse):
    rows = rows.astype(F32)
    ids = (rows[0:1, :] + rows[1:2, :] * BASE).astype(jnp.int32)
    return (iota((coarse, ids.shape[1]), 0) == ids).astype(F32).astype(BF16)


def own_onehot(sz, parent_ref):
    spread = idiv(iota((sz.blocks, sz.tokens), 1), BLK) == iota((sz.blocks, sz.tokens), 0)
    rows = mm(digits(parent_ref), spread.astype(F32).astype(BF16))
    return onehot_ids(rows, sz.coarse)


def fill_summary(sz, table, refs):
    mx = lax.axis_index("fx")
    for s, ref in enumerate(refs):
        start = pl.multiple_of((mx ^ s) * sz.owned, sz.owned)
        table[pl.ds(start, sz.owned), :] = ref[0 : sz.owned, :]


def prep_kernel(sz, fine, parent, cot, weight, *refs):
    outs, total, held = refs[: sz.nx + sz.ny], refs[-2], refs[-1]
    mx, my = lax.axis_index("fx"), lax.axis_index("fy")
    width = sz.width
    both = digits(parent)
    held[:, 0:width] = fine[...]
    held[:, width:] = mm(cot[...], weight[...], 1, 1).astype(BF16)

    def finish(out, tokens, block):
        onehot = (block == iota((sz.blocks, tokens), 0)).astype(F32).astype(BF16)
        out[tokens : tokens + PAD, :] = jnp.zeros((PAD, width + sz.half), BF16)
        out[tokens : tokens + PAD, 0:tokens] = mm(both, onehot).astype(BF16)

    for s in range(sz.ny):
        group, out, n = my ^ s, outs[sz.nx + s], sz.col_tokens
        place = place_col(sz, group)
        out[0:n, 0:width] = mm(place, held[:, 0:width]).astype(BF16)
        out[0:n, width:] = mm(place, held[:, width + sz.half :]).astype(BF16)
        t = iota((sz.blocks, n), 1)
        column = idiv(t, sz.rows) + group * sz.col_lines
        finish(out, n, imod(t, sz.rows) * (sz.columns // BLK) + idiv(column, BLK))
    for s in range(sz.nx):
        start, out, n = (mx ^ s) * sz.row_tokens, outs[s], sz.row_tokens
        out[0:n, :] = held[pl.ds(pl.multiple_of(start, n), n), 0 : width + sz.half]
        finish(out, n, idiv(iota((sz.blocks, n), 1) + start, BLK))
    total[...] = mm(own_onehot(sz, parent), cot[...])


def attend_kernel(sz, n, seg, offset, joined, last, *refs):
    refs = list(refs)

    def take(count):
        out = refs[:count]
        del refs[:count]
        return out

    pieces, tables = take(n), take(sz.nx)
    gain_ref, weight = take(2)
    before = take(3 if last else 0)
    o_outs, f_outs = take(n), take(0 if joined else n)
    keep, send = take(2)
    sums_outs = take(sz.nx if last else 2)
    table, xs, nb, gs, qkv, dqkv, os, fs, dw = take(9)
    tp, width, half = sz.tokens // n, sz.width, sz.half
    head = width // HEADS
    scale = head**-0.5
    lines = max(1, min(GROUP // (seg * n), tp // seg))
    part = lines * seg
    size = part * n
    groups = tp // part
    gain = gain_ref[...]

    fill_summary(sz, table, tables)
    onehots = []
    for p in range(n):
        onehot = onehot_ids(pieces[p][tp : tp + PAD, 0:tp], sz.coarse)
        onehots.append(onehot)
        x = pieces[p][0:tp, 0:width].astype(F32) + mm(onehot, table[...], 0, 0)
        for g in range(groups):
            at = g * size + p * part
            xs[at : at + part, :] = x[g * part : (g + 1) * part, :]
            gs[at : at + part, :] = pieces[p][g * part : (g + 1) * part, width:]
    x = xs[0 : sz.tokens, :]
    inv = lax.rsqrt(jnp.mean(x * x, axis=-1, keepdims=True) + 1e-06)
    nb[...] = (x * inv * gain).astype(BF16)
    for which in range(3):
        lo = which * width + offset
        qkv[:, which * half : (which + 1) * half] = mm(
            nb[...], weight[:, lo : lo + half]
        ).astype(BF16)

    row_line = idiv(imod(iota((size, size), 0), part), seg)
    col_line = idiv(imod(iota((size, size), 1), part), seg)
    bias = jnp.where(row_line == col_line, 0.0, -1e30).astype(F32)
    pair = 2 * head
    first = iota((size, pair), 1) < head
    lane = iota((1, pair), 1) < head
    masks = (lane.astype(F32).astype(BF16), 1 - lane.astype(F32).astype(BF16))
    for g in range(groups):
        at = slice(g * size, (g + 1) * size)
        for h in range(half // pair):
            cols = [slice(w * half + h * pair, w * half + (h + 1) * pair) for w in range(3)]
            q, k, v = (qkv[at, c] for c in cols)
            go = gs[at, cols[0]]
            res = []
            for m in masks:
                s = mm(q * m, k, 1, 1) * scale + bias
                e = jnp.exp(s - jnp.max(s, axis=-1, keepdims=True))
                w = e * (1.0 / jnp.sum(e, axis=-1, keepdims=True))
                wb = w.astype(BF16)
                gw = mm(go * m, v, 1, 1)
                inner = jnp.sum(w * gw, axis=-1, keepdims=True)
                ds = (w * (gw - inner) * scale).astype(BF16)
                res.append((mm(wb, v), mm(ds, k), mm(ds, q, 0, 0), mm(wb, go, 0, 0)))
            out = [jnp.where(first, a, b).astype(BF16) for a, b in zip(*res)]
            os[at, cols[0]] = out[0]
            for c, d in zip(cols, out[1:]):
                dqkv[at, c] = d

    gn = jnp.zeros((sz.tokens, width), F32)
    for which in range(3):
        lo = which * width + offset
        gn += mm(
            dqkv[:, which * half : (which + 1) * half], weight[:, lo : lo + half], 1, 1
        )
    pre = xs[0 : sz.tokens, :] * inv
    gain_sum = jnp.sum(gn * pre, axis=0, keepdims=True)
    gp = gn * gain
    fs[...] = (inv * (gp - pre * jnp.mean(gp * pre, axis=-1, keepdims=True))).astype(BF16)
    total = jnp.zeros((sz.coarse, width), F32)
    for p in range(n):
        for g in range(groups):
            at = g * size + p * part
            rows = slice(g * part, (g + 1) * part)
            o_outs[p][rows, 0:half] = os[at : at + part, :]
            if joined:
                o_outs[p][rows, half:] = fs[at : at + part, :]
            else:
                f_outs[p][rows, :] = fs[at : at + part, :]
        total += mm(onehots[p], o_outs[p][:, half:] if joined else f_outs[p][...])
    dw[...] = mm(nb[...], dqkv[...], 0, 0)
    split_blocks(sz, dw, keep, send)
    if not last:
        sums_outs[0][...] = total
        sums_outs[1][...] = gain_sum
        return
    xs[0 : sz.coarse, :] = total + before[0][...] + before[1][...]
    small = coarse_terms(sz, tables, xs, gain_sum + before[2][...], sums_outs)
    for out in (keep, send):
        out[width // 2 :, 0:width] = small
        out[width // 2 :, width:] = jnp.zeros((PAD, 3 * half - width), BF16)


def split_blocks(sz, dw, keep, send):
    rows = dw.shape[0] // sz.nd
    bit = lax.axis_index("dp") & 1
    for j in range(sz.nd // 2):
        for out, b in ((keep, bit), (send, 1 - bit)):
            start = pl.multiple_of((2 * j + b) * rows, rows)
            out[j * rows : (j + 1) * rows, :] = dw[pl.ds(start, rows), :].astype(BF16)


def mix_kernel(sz, fine, parent, cot, weight, *refs):
    tables, refs = refs[: sz.nx], refs[sz.nx :]
    row_out, refs = refs[: sz.nx], refs[sz.nx :]
    col_out, refs = refs[: sz.ny], refs[sz.ny :]
    mixed, keep, send, table, att, dw = refs
    my = lax.axis_index("fy")
    mx = lax.axis_index("fx")
    fill_summary(sz, table, tables)
    for s in range(sz.nx):
        start = pl.multiple_of((mx ^ s) * sz.row_tokens, sz.row_tokens)
        att[pl.ds(start, sz.row_tokens), 0 : sz.half] = row_out[s][:, 0 : sz.half]
    col = jnp.zeros((sz.tokens, sz.half), F32)
    for s in range(sz.ny):
        col += mm(place_col(sz, my ^ s, True), col_out[s][...])
    att[:, sz.half :] = col.astype(BF16)
    x = fine[...].astype(F32) + mm(own_onehot(sz, parent), table[...], 0, 0)
    mixed[...] = (x + mm(att[...], weight[...])).astype(BF16)
    dw[...] = mm(att[...], cot[...], 0, 0)
    split_blocks(sz, dw, keep, send)


def tokens_kernel(sz, cot, *refs):
    rows, refs = refs[: sz.nx], refs[sz.nx :]
    cols, refs = refs[: sz.ny], refs[sz.ny :]
    out, held = refs
    my, mx = lax.axis_index("fy"), lax.axis_index("fx")
    for s in range(sz.nx):
        start = pl.multiple_of((mx ^ s) * sz.row_tokens, sz.row_tokens)
        held[pl.ds(start, sz.row_tokens), :] = rows[s][:, sz.half :]
    total = held[...].astype(F32) + cot[...].astype(F32)
    for s in range(sz.ny):
        total += mm(place_col(sz, my ^ s, True), cols[s][...])
    out[...] = total.astype(BF16)


def pick(stack, index):
    return lax.dynamic_index_in_dim(stack, index, 0, keepdims=False)


def after(value, *others):
    return lax.optimization_barrier((value, others))[0]


def reduce_steps(keep, send, nd, extra=0):
    md = lax.axis_index("dp")
    n, me = lax.axis_size("fx"), lax.axis_index("fx")
    columns = keep.shape[-1]
    rows = (keep.shape[0] - extra) // (nd // 2)
    state = {}

    def cut(value, *shape):
        body = value.shape[0] - extra
        return value[:body].reshape(*shape, columns), value[body:]

    def with_tail(body, tail):
        body = body.reshape(-1, columns)
        return jnp.concatenate([body, tail], axis=0) if extra else body

    def first(*deps):
        state["v"] = tree([keep, xor_send(after(send, *deps), "dp", 1)])
        return state["v"]

    def halve(step, *deps):
        bit = (md // step) & 1
        parts, tail = cut(after(state["v"], *deps), -1, 2, rows)
        other = lax.dynamic_index_in_dim(parts, 1 - bit, 1, keepdims=False)
        mine = lax.dynamic_index_in_dim(parts, bit, 1, keepdims=False)
        state["v"] = tree([with_tail(mine, tail), xor_send(with_tail(other, tail), "dp", step)])
        return state["v"]

    def spread(*deps):
        parts, tail = cut(after(state["v"], *deps), n, rows // n)
        got = [xor_send(with_tail(pick(parts, me ^ s), tail), "fx", s) for s in range(1, n)]
        state["v"] = tree([with_tail(pick(parts, me), tail)] + got)
        return state["v"]

    def double(step, *deps):
        value = after(state["v"], *deps)
        state["v"] = tree([value, xor_send(value, "fy", step)])
        return state["v"]

    def gather(*deps):
        value, tail = cut(after(state["v"], *deps), rows // n)
        got = [value] + [xor_send(value, "fx", s) for s in range(1, n)]
        ordered = []
        for j in range(n):
            piece = got[j]
            for m in range(1, n):
                piece = jnp.where(me == m, got[j ^ m], piece)
            ordered.append(piece)
        return jnp.concatenate(ordered, axis=0), tail

    steps = [first]
    step = 2
    while step < nd:
        steps.append(functools.partial(halve, step))
        step *= 2
    steps.append(spread)
    step = 1
    while step < lax.axis_size("fy"):
        steps.append(functools.partial(double, step))
        step *= 2
    return steps + [gather]


def coarse_terms(sz, tables, total, gain, outs):
    mx = lax.axis_index("fx")
    levels = jnp.zeros((PAD, sz.width), F32)
    for s in range(sz.nx):
        mine = total[pl.ds(pl.multiple_of((mx ^ s) * sz.owned, sz.owned), sz.owned), :]
        high = mine.astype(BF16)
        low = (mine - high.astype(F32)).astype(BF16)
        level = tables[s][sz.owned : sz.owned + PAD, 0 : sz.owned][0:1, :].astype(F32)
        onehot = (iota((PAD, sz.owned), 0) == level.astype(jnp.int32)).astype(F32).astype(BF16)
        levels += mm(onehot, high) + mm(onehot, low)
        outs[s][...] = high
    row_id = iota((PAD, sz.width), 0)
    return jnp.where(
        row_id < LEVELS, levels, jnp.where(row_id == LEVELS, gain, 0.0)
    ).astype(BF16)


def tree(terms):
    terms = [t.astype(F32) for t in terms]
    while len(terms) > 1:
        terms = [a + b for a, b in zip(terms[0::2], terms[1::2])]
    return terms[0].astype(BF16)


def coarse_steps(sums, ny):
    state = {}

    def spread(*deps):
        parts = after(sums, *deps)
        got = [xor_send(parts[s], "fx", s) for s in range(1, len(parts))]
        state["v"] = tree([parts[0]] + got)
        return state["v"]

    def double(step, *deps):
        value = after(state["v"], *deps)
        state["v"] = tree([value, xor_send(value, "fy", step)])
        return state["v"]

    return [spread] + [functools.partial(double, 1 << i) for i in range(ny.bit_length() - 1)]


def local(
    fine_tokens,
    parent,
    coarse_tokens,
    tile_level,
    level_table,
    norm_gain,
    qkv_weight,
    out_weight,
    cotangent,
):
    frames, rows, columns, width = fine_tokens.shape
    owned = coarse_tokens.shape[1]
    sz = Sizes(rows, columns, width, owned)
    nx, ny, nd, tokens, half, coarse = sz.nx, sz.ny, sz.nd, sz.tokens, sz.half, sz.coarse
    if frames != 1 or not all(is_power(n) for n in (nx, ny, nd)):
        raise ValueError("unsupported mesh")

    def out(shape, dtype=BF16):
        return jax.ShapeDtypeStruct(shape, dtype)

    def vmem(shape, dtype=BF16):
        return pltpu.VMEM(shape, dtype)

    fine = fine_tokens.reshape(tokens, width)
    cot = cotangent.reshape(tokens, width)
    parents = parent.reshape(1, sz.blocks)
    gain = norm_gain.reshape(1, width)
    tr, tc = sz.row_tokens, sz.col_tokens

    level_onehot = (tile_level[0, :, None] == jnp.arange(LEVELS, dtype=jnp.int32)).astype(F32)
    level_add = jnp.sum(level_onehot[:, :, None] * level_table[None, :, :], axis=1)
    summary = (coarse_tokens[0].astype(F32) + level_add).astype(BF16)
    levels = jnp.pad(tile_level.astype(BF16), ((0, PAD - 1), (0, width - owned)))
    summary = jnp.concatenate([summary, levels], axis=0)
    *sent, cot_sums = call(
        functools.partial(prep_kernel, sz),
        [out((tr + PAD, width + half))] * nx
        + [out((tc + PAD, width + half))] * ny
        + [out((coarse, width), F32)],
        [vmem((tokens, 2 * width))],
        (4 * tokens * width * 2 * width, 10 * tokens * width),
        "prep",
        fine,
        parents,
        cot,
        out_weight,
    )
    tables = [summary] + [xor_send(summary, "fx", s) for s in range(1, nx)]
    row_in = [sent[0]] + [xor_send(sent[s], "fx", s) for s in range(1, nx)]
    col_in = [sent[nx]] + [xor_send(sent[nx + s], "fy", s) for s in range(1, ny)]

    def attend(n, seg, offset, joined, pieces, name, before=()):
        tp = tokens // n
        pair = [out((tp, half + width))] * n
        apart = [out((tp, half))] * n + [out((tp, width))] * n
        sums = [out((owned, width))] * nx
        if not before:
            sums = [out((coarse, width), F32), out((1, width), F32)]
        dw_rows = width // 2 + (PAD if before else 0)
        res = call(
            functools.partial(attend_kernel, sz, n, seg, offset, joined, bool(before)),
            (pair if joined else apart) + [out((dw_rows, 3 * half))] * 2 + sums,
            [
                vmem((coarse, width)),
                vmem((max(tokens, coarse), width), F32),
                vmem((tokens, width)),
                vmem((tokens, half)),
                vmem((tokens, 3 * half)),
                vmem((tokens, 3 * half)),
                vmem((tokens, half)),
                vmem((tokens, width)),
                vmem((width, 3 * half), F32),
            ],
            (10 * tokens * width * 3 * width, 12 * tokens * width),
            name,
            *pieces,
            *tables,
            gain,
            qkv_weight,
            *before,
        )
        back, res = (res[:n], res[n:]) if joined else (res[: 2 * n], res[2 * n :])
        return back, res[:2], res[2:]

    row_of, row_w, row_sums = attend(nx, columns, 0, True, row_in, "row_heads")
    row_of = [row_of[0]] + [xor_send(row_of[s], "fx", s) for s in range(1, nx)]
    row_steps = reduce_steps(*row_w, nd)
    row_steps[0]()

    col_in = after(col_in, row_sums)
    col_back, col_w, sums = attend(
        ny, rows, half, False, col_in, "col_heads", (cot_sums, *row_sums)
    )
    col_o, col_f = col_back[:ny], col_back[ny:]
    col_o = [col_o[0]] + [xor_send(col_o[s], "fy", s) for s in range(1, ny)]
    col_f = [col_f[0]] + [xor_send(col_f[s], "fy", s) for s in range(1, ny)]
    col_steps = reduce_steps(*col_w, nd, PAD)
    sum_steps = coarse_steps(sums, ny)
    col_first = col_steps[0]()
    stage = [row_steps[1](), col_first, sum_steps[0]()]

    mixed, *out_w = call(
        functools.partial(mix_kernel, sz),
        [out((tokens, width))] + [out((width // 2, width))] * 2,
        [vmem((coarse, width)), vmem((tokens, width)), vmem((width, width), F32)],
        (4 * tokens * width * width, 10 * tokens * width),
        "mix",
        fine,
        parents,
        cot,
        out_weight,
        *tables,
        *row_of,
        *after(col_o, col_first),
    )
    out_steps = reduce_steps(*out_w, nd)
    chains = ((row_steps, 0), (col_steps, 1), (out_steps, 2), (sum_steps, 1))
    done = [None] * len(chains)
    for t in range(2, len(row_steps) + 2):
        now = []
        for c, (steps, lag) in enumerate(chains):
            if 0 <= t - lag < len(steps):
                now.append(steps[t - lag](*stage))
                done[c] = now[-1]
        stage = now
        if t == 2:
            col_f = after(col_f, *stage)
    (row_weight, _), (col_weight, small), (out_weight_sum, _), total = done
    grad_coarse, small = total.astype(F32), small[:, :width].astype(F32)

    grad_tokens = call(
        functools.partial(tokens_kernel, sz),
        [out((tokens, width))],
        [vmem((tokens, width))],
        (2 * tokens * tokens * width, 8 * tokens * width),
        "grad_tokens",
        cot,
        *row_of,
        *col_f,
    )[0]

    scale = 1.0 / math.sqrt(tokens * nd * nx * ny)
    parts = []
    for which in range(3):
        cols = slice(which * half, (which + 1) * half)
        parts += [row_weight[:, cols], col_weight[:, cols]]
    grad_qkv = jnp.concatenate(parts, axis=1).astype(F32) * scale
    gain_rows = small[LEVELS].reshape(nd, width // nd)
    return (
        mixed.reshape(fine_tokens.shape),
        grad_tokens.reshape(fine_tokens.shape),
        grad_coarse.reshape(1, owned, width),
        grad_qkv,
        out_weight_sum.astype(F32) * scale,
        pick(gain_rows, lax.axis_index("dp")) * scale,
        small[:LEVELS] * scale,
    )


def solution(mesh):
    return jax.shard_map(
        local,
        mesh=mesh,
        in_specs=(
            P("dp", "fy", "fx", None),
            P("dp", "fy", "fx"),
            P("dp", "fx", None),
            P("dp", "fx"),
            P(),
            P(),
            P(),
            P(),
            P("dp", "fy", "fx", None),
        ),
        out_specs=(
            P("dp", "fy", "fx", None),
            P("dp", "fy", "fx", None),
            P("dp", "fx", None),
            P("dp", None),
            P("dp", None),
            P("dp"),
            P(),
        ),
        check_vma=False,
    )
```
